512 devices in a mesh: row: 32 (over y, z_lo, core), col: 16 (over z_hi, x).
Axes of the slice: x: 4, y: 8, z: 8 (z_hi: 4, z_lo: 2; z = z_hi * 2 + z_lo), core: 2. Of those that a mesh axis runs over, the one named last changes fastest.
Arguments:
- modes: bfloat16 [3072, 1536, 128], P('row', 'col'), may hold values from -0.29882812 to 0.29882812
- conductivity: float32 [2560, 1280], P('row', 'col'), may hold values from 0.1 to 10
- storage: float32 [2560, 1280], P('row', 'col'), may hold values from 0.5 to 8
- owners: int32 [32, 16, 16, 1], P('row', 'col'), may hold values from 0 to 15; in each aligned block of 16 rows (0 to 15, 16 to 31, ..., all dimensions but the last counted through in order) at most 2 rows name the same one
Outputs:
- coarse_self: float32 [32, 512, 8, 128], P('row', 'col')
- coarse_cross: float32 [32, 512, 8, 8, 128], P('row', 'col')
The draws below stay inside these ranges and needn't reach their ends.
Inputs may be any that keep to these rules, and one draw needn't show every extreme that they name: Among the 16 entries owners[r, c, :, 0] of one subdomain no column appears more than 2 times, and some column appears exactly 2 times in some subdomain.
All inputs are finite; a program needn't handle non-finite values.
Results may differ from the reference program's by a relative error of at most 0.0046.
Values may be sent and summed in bfloat16 or wider, within the bound.
A program may use at most 64 MiB of HBM per device.

```python
import math
import jax
import jax.numpy as jnp
import numpy as np
from jax import lax

CELLS = 80
INTERSECTION = 8
MODES = 128
SWEEPS = 3
GROUPS = 16
SLOTS = 32
EXT = 96
FULL = 98
STRIP = 17
GROUP_ROWS = 8
MOST = 2
GRID_A = 2560
GRID_B = 1280
N_ROW = 32
N_COL = 16


def block_scale(key, shape, shards, low, top_value):
    def one(dim, blocks):
        steps = jax.random.uniform(jax.random.fold_in(jax.random.fold_in(key, 6), dim), (blocks,), jnp.float32, low / len(shards), top_value / len(shards))
        return jnp.repeat(jnp.exp(steps), shape[dim] // blocks).reshape((-1,) + (1,) * (len(shape) - dim - 1))

    gain = one(*shards[0])
    for cut in shards[1:]:
        gain = gain * one(*cut)
    return gain


def assign_block(stream_key, own, number, rows, amount, top, reach, slope):
    ranking = jax.random.permutation(stream_key, amount)
    heavy_load, usual = load_shares(amount, rows * top, reach, slope, True), load_shares(amount, rows * top, reach, slope, False)
    places = jnp.arange(amount)

    def named(sizes, offset_by):
        used = int((sizes > 0).sum())
        fixed = max(1, used // 4)
        moved = fixed + (places - fixed + offset_by * (used - fixed)) % max(1, amount - fixed)
        return jnp.zeros((amount,), jnp.int32).at[ranking[jnp.where(places < fixed, places, moved)]].set(jnp.asarray(sizes, jnp.int32))

    sizes = jnp.where(number % 4 == 0, named(heavy_load, number // 4), named(usual, number - number // 4 - 1))
    mixed = jax.random.permutation(jax.random.fold_in(own, 3), amount)
    source_of, receiver = mixed[0:amount // 2 * 2:2], mixed[1:amount // 2 * 2:2]
    room = jnp.minimum(sizes[source_of] - 1, reach - sizes[receiver]) // 2
    room = jnp.where((source_of == ranking[0]) | (receiver == ranking[0]) | (sizes[receiver] == 0), 0, jnp.maximum(room, 0))
    moved = jax.random.randint(jax.random.fold_in(own, 4), (amount // 2,), 0, 1 << 20) % (room + 1)
    sizes = sizes.at[source_of].add(-moved).at[receiver].add(moved)
    labels = jnp.searchsorted(jnp.cumsum(sizes), jnp.arange(rows * top), side="right").astype(jnp.int32)
    listing = labels.reshape(top, rows).T
    listing = listing[jax.random.permutation(jax.random.fold_in(own, 1), rows)]
    offset_by = jax.random.randint(jax.random.fold_in(own, 2), (rows, 1), 0, top)
    return jnp.take_along_axis(listing, (jnp.arange(top)[None, :] + offset_by) % top, axis=1)


def load_shares(number_of, total, reach, lean, full):
    loads = [(1 << 20) // math.isqrt(standing ** lean) + 1 for standing in range(1, number_of + 1)]
    largest = reach if full else min(reach, max(-(-total // number_of), total * loads[0] // sum(loads)))
    least = 1 if total - largest >= number_of - 1 else 0
    counts, surplus = [largest] + [least] * (number_of - 1), total - largest - least * (number_of - 1)
    while surplus > 0:
        movable = [i for i in range(1, number_of) if counts[i] < largest] or [i for i in range(1, number_of) if counts[i] < reach]
        pool, left = sum([loads[i] for i in movable]), surplus
        for i in movable:
            addition = min(reach - counts[i], max(1, left * loads[i] // pool), surplus)
            counts[i] = counts[i] + addition
            surplus = surplus - addition
    return np.array(counts)


def normal_values(own_key, shape, spread, limit, pieces=(), kind=jnp.bfloat16):
    entries = jax.random.normal(own_key, shape, jnp.float32) * spread
    if len(pieces) > 0:
        entries = block_scale(own_key, shape, pieces, -0.22, 0.18) * entries
    return jnp.clip(entries, min=-limit, max=limit).astype(kind)


def setup_inputs(seed: int = 0) -> dict:
    arg_keys = jax.random.split(jax.random.key(seed), 5)
    modes = normal_values(arg_keys[0], (EXT * N_ROW, EXT * N_COL, MODES), 0.05, 0.29882812, ((0, 32), (1, 16)))
    conductivity = jnp.clip(jnp.exp(math.log(10.0) - 4.6051702 * jax.random.uniform(arg_keys[1], (GRID_A, GRID_B), jnp.float32) ** block_scale(arg_keys[1], (GRID_A, GRID_B), ((0, 32), (1, 16)), -0.2, 0.2)), 0.1, 10.0)
    storage = jnp.clip(jnp.exp(math.log(8.0) - 2.7725887 * jax.random.uniform(arg_keys[2], (GRID_A, GRID_B), jnp.float32) ** block_scale(arg_keys[2], (GRID_A, GRID_B), ((0, 32), (1, 16)), -0.2, 0.2)), 0.5, 8.0)
    owners_keys = jax.random.split(jax.random.fold_in(arg_keys[3], 1), N_ROW * N_COL * GROUPS // GROUPS)
    owners_turns = jax.random.permutation(jax.random.fold_in(arg_keys[3], 3), N_ROW * N_COL * GROUPS // GROUPS)
    owners = jax.vmap(lambda own, number: assign_block(jax.random.fold_in(arg_keys[3], 2), own, number, GROUPS, N_COL, 1, MOST, 2))(owners_keys, owners_turns).reshape((N_ROW, N_COL, GROUPS, 1))
    return dict(modes=modes, conductivity=conductivity, storage=storage, owners=owners)


stencil_offsets = ((-1, -1, 0.5), (-1, 0, 1.0), (-1, 1, 0.5), (0, -1, 1.0), (0, 1, 1.0), (1, -1, 0.5), (1, 0, 1.0), (1, 1, 0.5))
pair_offsets = ((1, 0), (0, 1), (1, 1), (1, -1))


def chebyshev_weights(count):
    return [1.0 / (1.15 + 0.85 * math.cos(math.pi * (2 * position + 1) / (2 * count))) for position in range(count)]


def couplings(coefficient):
    size_a = coefficient.shape[0] - 2
    size_b = coefficient.shape[1] - 2
    center = coefficient[1:size_a + 1, 1:size_b + 1]
    result = []
    for shift_a, shift_b, factor in stencil_offsets:
        result.append(factor * 0.5 * (center + coefficient[1 + shift_a:size_a + 1 + shift_a, 1 + shift_b:size_b + 1 + shift_b]))
    return result


def apply_operator(source_field, weights, diagonal):
    size_a = diagonal.shape[0]
    size_b = diagonal.shape[1]
    accumulated = diagonal[:, :, None] * source_field[1:size_a + 1, 1:size_b + 1]
    for (shift_a, shift_b, factor), weight in zip(stencil_offsets, weights):
        accumulated = accumulated - weight[:, :, None] * source_field[1 + shift_a:size_a + 1 + shift_a, 1 + shift_b:size_b + 1 + shift_b]
    return accumulated


def smooth_and_apply(mode_tile, conduct_tile, storage_tile, inside_tile, sweep_count):
    weights_f = couplings(jnp.pad(conduct_tile, 1))
    diagonal_f = storage_tile + sum(weights_f)
    weights_e = [weight[1:-1, 1:-1] for weight in weights_f]
    diagonal_e = diagonal_f[1:-1, 1:-1]
    inside_e = inside_tile[1:-1, 1:-1]
    inverse = inside_e / (diagonal_e + 1.0 - inside_e)
    current = mode_tile.astype(jnp.float32) * inside_e[:, :, None]
    for omega in chebyshev_weights(sweep_count):
        applied = apply_operator(jnp.pad(current, ((1, 1), (1, 1), (0, 0))), weights_e, diagonal_e)
        current = current - omega * (inverse[:, :, None] * applied)
    smoothed = lax.optimization_barrier(current.astype(jnp.bfloat16))
    image = apply_operator(jnp.pad(smoothed.astype(jnp.float32), ((2, 2), (2, 2), (0, 0))), weights_f, diagonal_f)
    return smoothed, image.astype(jnp.bfloat16)


def pair_block(first_tile, second_tile):
    first_flat = first_tile.reshape(-1, first_tile.shape[2])
    second_flat = second_tile.reshape(-1, second_tile.shape[2])
    return lax.dot_general(first_flat, second_flat, (((0,), (0,)), ((), ())), preferred_element_type=jnp.float32)


def mode_region(smoothed, pair_kind, cell_count, strip_width):
    extent = smoothed.shape[0]
    if pair_kind == 0:
        return smoothed[cell_count - 1:extent, :]
    if pair_kind == 1:
        return smoothed[:, cell_count - 1:extent]
    if pair_kind == 2:
        return smoothed[cell_count - 1:extent, cell_count - 1:extent]
    return smoothed[cell_count - 1:extent, 0:strip_width]


def image_region(image, pair_kind, strip_width):
    full_size = image.shape[0]
    if pair_kind == 0:
        return image[0:strip_width, 1:full_size - 1]
    if pair_kind == 1:
        return image[1:full_size - 1, 0:strip_width]
    if pair_kind == 2:
        return image[0:strip_width, 0:strip_width]
    return image[0:strip_width, full_size - strip_width:full_size]


def shifted(grid_blocks, shift_a, shift_b):
    padded = jnp.pad(grid_blocks, ((1, 1), (1, 1)) + ((0, 0),) * (grid_blocks.ndim - 2))
    return padded[1 - shift_a:1 - shift_a + grid_blocks.shape[0], 1 - shift_b:1 - shift_b + grid_blocks.shape[1]]


def reference(modes, conductivity, storage, owners):
    margin = INTERSECTION + 1
    conduct_pad = jnp.pad(conductivity, margin)
    storage_pad = jnp.pad(storage, margin)
    inside_pad = jnp.pad(jnp.ones((GRID_A, GRID_B), jnp.float32), margin)
    subdomain_ids = jnp.arange(N_ROW * N_COL, dtype=jnp.int32)

    def first_pass(flat_id):
        row_id = (flat_id // N_COL).astype(jnp.int32)
        col_id = (flat_id % N_COL).astype(jnp.int32)
        zero_index = jnp.int32(0)
        mode_tile = lax.dynamic_slice(modes, ((row_id * EXT).astype(jnp.int32), (col_id * EXT).astype(jnp.int32), zero_index), (EXT, EXT, MODES))
        start_a = (row_id * CELLS).astype(jnp.int32)
        start_b = (col_id * CELLS).astype(jnp.int32)
        conduct_tile = lax.dynamic_slice(conduct_pad, (start_a, start_b), (FULL, FULL))
        storage_tile = lax.dynamic_slice(storage_pad, (start_a, start_b), (FULL, FULL))
        inside_tile = lax.dynamic_slice(inside_pad, (start_a, start_b), (FULL, FULL))
        smoothed, image = smooth_and_apply(mode_tile, conduct_tile, storage_tile, inside_tile, SWEEPS)
        self_block = pair_block(smoothed, image[1:-1, 1:-1])
        image_parts = tuple(image_region(image, pair_kind, STRIP) for pair_kind in range(4))
        return smoothed, self_block, image_parts

    smoothed_all, self_all, image_parts = lax.map(first_pass, subdomain_ids)

    def second_pass(flat_id):
        row_id = flat_id // N_COL
        col_id = flat_id % N_COL
        own_modes = smoothed_all[flat_id]
        formed = []
        for pair_kind in range(4):
            shift_a, shift_b = pair_offsets[pair_kind]
            other_row = row_id + shift_a
            other_col = col_id + shift_b
            valid = (other_row < N_ROW) & (other_col >= 0) & (other_col < N_COL)
            other_id = (jnp.clip(other_row, 0, N_ROW - 1) * N_COL + jnp.clip(other_col, 0, N_COL - 1)).astype(jnp.int32)
            block = pair_block(mode_region(own_modes, pair_kind, CELLS, STRIP), image_parts[pair_kind][other_id])
            formed.append(jnp.where(valid, block, jnp.zeros_like(block)))
        return jnp.stack(formed)

    formed_all = lax.map(second_pass, subdomain_ids).reshape(N_ROW, N_COL, 4, MODES, MODES)
    transposed = jnp.swapaxes(formed_all, -1, -2)
    cross_rows = jnp.stack([
        shifted(transposed[:, :, 2], 1, 1),
        shifted(transposed[:, :, 0], 1, 0),
        shifted(transposed[:, :, 3], 1, -1),
        shifted(transposed[:, :, 1], 0, 1),
        formed_all[:, :, 1],
        formed_all[:, :, 3],
        formed_all[:, :, 0],
        formed_all[:, :, 2]], axis=2)
    self_groups = self_all.reshape(N_ROW, N_COL, GROUPS, GROUP_ROWS, MODES)
    cross_groups = cross_rows.reshape(N_ROW, N_COL, 8, GROUPS, GROUP_ROWS, MODES).transpose(0, 1, 3, 2, 4, 5)
    destination = owners[:, :, :, 0]
    chosen = (destination[:, :, :, None] == jnp.arange(N_COL, dtype=jnp.int32)[None, None, None, :]).astype(jnp.int32)
    earlier = jnp.cumsum(chosen, axis=2) - chosen
    rank_in = jnp.sum(earlier * chosen, axis=3)
    col_ids = jnp.broadcast_to(jnp.arange(N_COL, dtype=jnp.int32)[None, :, None], destination.shape)
    row_ids = jnp.broadcast_to(jnp.arange(N_ROW, dtype=jnp.int32)[:, None, None], destination.shape)
    slot_ids = (destination * SLOTS + col_ids * MOST + rank_in).astype(jnp.int32)
    coarse_self = jnp.zeros((N_ROW, N_COL * SLOTS, GROUP_ROWS, MODES), jnp.float32).at[row_ids, slot_ids].set(self_groups)
    coarse_cross = jnp.zeros((N_ROW, N_COL * SLOTS, 8, GROUP_ROWS, MODES), jnp.float32).at[row_ids, slot_ids].set(cross_groups)
    return coarse_self, coarse_cross
```

```python
import functools
import math

import jax
import jax.numpy as jnp
from jax import lax
from jax.experimental import pallas as pl
from jax.experimental.pallas import tpu as pltpu
from jax.sharding import PartitionSpec as P

CELLS = 80
EXT = 96
MODES = 128
SWEEPS = 3
GROUPS = 16
FRAME = 112
CHUNK = 32
MESH = pl.DeviceIdType.MESH
F32 = jnp.float32
BF16 = jnp.bfloat16
PAIRS = ((1, 0), (0, 1), (1, 1), (1, -1))
VMEM = pl.BlockSpec(memory_space=pltpu.VMEM)
SMEM = pl.BlockSpec(memory_space=pltpu.SMEM)


def neighbour(da, db):
    rows, cols = lax.axis_size("row"), lax.axis_size("col")
    r, c = lax.axis_index("row"), lax.axis_index("col")
    return (lax.rem(r + da + rows, rows), lax.rem(c + db + cols, cols))


AROUND = tuple((a, b) for a in (-1, 0, 1) for b in (-1, 0, 1) if (a, b) != (0, 0))


def greet(others):
    barrier = pltpu.get_barrier_semaphore()
    for device in others:
        pl.semaphore_signal(barrier, inc=1, device_id=device, device_id_type=MESH)
    pl.semaphore_wait(barrier, len(others))


def lanes(shape):
    return lax.broadcasted_iota(jnp.int32, shape, 1)


def halo_kernel(k_ref, s_ref, out_ref, mid, side, left, right, send, recv):
    rows, cols = lax.axis_size("row"), lax.axis_size("col")
    r, c = lax.axis_index("row"), lax.axis_index("col")
    own = []
    for ref in (k_ref, s_ref):
        own.append(
            jnp.concatenate(
                [jnp.zeros((CELLS, 16), F32), ref[...], jnp.zeros((CELLS, 32), F32)], axis=1
            )
        )
    k, s = own
    lane = lanes((CELLS, 128))
    mid[0, 16:96, :] = k
    mid[1, 16:96, :] = s
    packed = jnp.where(lane < 64, pltpu.roll(s, 96, 1), 0.0)
    packed = jnp.where(lane < 48, pltpu.roll(k, 80, 1), packed)
    packed = jnp.where(lane < 32, s, packed)
    packed = jnp.where(lane < 16, pltpu.roll(k, 112, 1), packed)
    side[...] = packed
    greet([neighbour(a, b) for a, b in AROUND])
    plan = [
        ((-1, 0), mid.at[:, 16:32, :], mid.at[:, 96:112, :]),
        ((1, 0), mid.at[:, 80:96, :], mid.at[:, 0:16, :]),
        ((0, -1), side, right.at[16:96, :]),
        ((0, 1), side, left.at[16:96, :]),
        ((-1, -1), side.at[0:16, :], right.at[96:112, :]),
        ((-1, 1), side.at[0:16, :], left.at[96:112, :]),
        ((1, -1), side.at[64:80, :], right.at[0:16, :]),
        ((1, 1), side.at[64:80, :], left.at[0:16, :]),
    ]
    copies = []
    for n, ((a, b), src, dst) in enumerate(plan):
        copy = pltpu.make_async_remote_copy(
            src_ref=src,
            dst_ref=dst,
            send_sem=send.at[n],
            recv_sem=recv.at[n],
            device_id=neighbour(a, b),
            device_id_type=MESH,
        )
        copy.start()
        copies.append(copy)
    for copy in copies:
        copy.wait()
    lane = lanes((FRAME, 128))
    line = lax.broadcasted_iota(jnp.int32, (FRAME, 128), 0)
    first_a, last_a = jnp.where(r == 0, 16, 0), jnp.where(r == rows - 1, 96, FRAME)
    first_b, last_b = jnp.where(c == 0, 16, 0), jnp.where(c == cols - 1, 96, FRAME)
    inside = (line >= first_a) & (line < last_a) & (lane >= first_b) & (lane < last_b)
    low, high = left[...], right[...]
    for n, (shift_low, shift_high) in enumerate(((96, 96), (80, 80))):
        whole = jnp.where(lane < 96, mid[n], pltpu.roll(high, shift_high, 1))
        whole = jnp.where(lane < 16, pltpu.roll(low, shift_low, 1), whole)
        out_ref[n] = jnp.where(inside, whole, 0.0)
    out_ref[2] = inside.astype(F32)


def around(conductivity, storage):
    return pl.pallas_call(
        halo_kernel,
        out_shape=jax.ShapeDtypeStruct((3, FRAME, 128), F32),
        in_specs=[VMEM, VMEM],
        out_specs=VMEM,
        scratch_shapes=[
            pltpu.VMEM((2, FRAME, 128), F32),
            pltpu.VMEM((CELLS, 128), F32),
            pltpu.VMEM((FRAME, 128), F32),
            pltpu.VMEM((FRAME, 128), F32),
            pltpu.SemaphoreType.DMA((8,)),
            pltpu.SemaphoreType.DMA((8,)),
        ],
        compiler_params=pltpu.CompilerParams(collective_id=0, has_side_effects=True),
    )(conductivity, storage)


def omegas():
    return [
        1.0 / (1.15 + 0.85 * math.cos(math.pi * (2 * t + 1) / (2 * SWEEPS))) for t in range(SWEEPS)
    ]


def across(ref, line, start):
    low = ref[line, pl.ds(start - 1, CHUNK), :]
    mid = ref[line, pl.ds(pl.multiple_of(start, 8), CHUNK), :]
    high = ref[line, pl.ds(start + 1, CHUNK), :]
    return mid, (low + high) + (mid + mid)


def walk(z_ref, q_ref, first, last, unroll, body):
    @pl.loop(0, EXT // CHUNK)
    def _(chunk):
        start = 8 + chunk * CHUNK
        zc, hz = across(z_ref, first, start)
        qc, hq = across(q_ref, first, start)
        _, hz0 = across(z_ref, first - 1, start)
        _, hq0 = across(q_ref, first - 1, start)

        def step(line, carry):
            zc, hz, pz, qc, hq, pq = carry
            zn, hzn = across(z_ref, line + 1, start)
            qn, hqn = across(q_ref, line + 1, start)
            pzn, pqn = hz + hzn, hq + hqn
            body(line, start, zc, qc, pz + pzn, pq + pqn)
            return zn, hzn, pzn, qn, hqn, pqn

        lax.fori_loop(
            first, last, step, (zc, hz, hz0 + hz, qc, hq, hq0 + hq), unroll=unroll
        )


def smooth_kernel(
    coef_ref, modes_ref, owners_ref,
    row_s, row_i, col_s, col_i, edges, corners, self_ref, place_ref,
    kb, gb, db, za, qa, zb, qb, s_all, i_all,
):
    k, s, inside = coef_ref[0], coef_ref[1], coef_ref[2]
    kp = jnp.concatenate([k, jnp.zeros((128 - FRAME, 128), F32)], axis=0)

    def three(x, axis):
        return pltpu.roll(x, 1, axis) + pltpu.roll(x, 127, axis) + 2.0 * x

    total = three(three(kp, 0), 1)[:FRAME]
    diagonal = s + 2.0 * k + 0.25 * total
    inverse = inside / (diagonal + (1.0 - inside))
    columns = []
    for x in (k, inverse, diagonal):
        xp = jnp.concatenate([x, jnp.zeros((128 - FRAME, 128), F32)], axis=0)
        columns.append(xp.T[8 : 8 + EXT])
    omega = omegas()
    scale = 1.0
    for w in omega:
        scale = scale * w / 4.0
    edge = jnp.zeros((8, MODES), F32)
    for ref in (za, qa, zb, qb):
        for line in (0, 1, EXT + 2, EXT + 3):
            ref[line] = jnp.zeros((FRAME, MODES), F32)
    for line in range(2, EXT + 2):
        for ref in (za, qa, zb, qb):
            ref[line, 0:8, :] = edge
            ref[line, 104:112, :] = edge
    for line in range(1, EXT + 3):
        at = line + 6
        kx = jnp.broadcast_to(columns[0][:, at : at + 1], (EXT, MODES))
        kb[line] = kx
        if 2 <= line < EXT + 2:
            gx = jnp.broadcast_to(columns[1][:, at : at + 1], (EXT, MODES))
            gb[line] = gx
            db[line] = jnp.broadcast_to(columns[2][:, at : at + 1], (EXT, MODES))
            z = jnp.where(gx > 0.0, modes_ref[line - 2].astype(F32) * scale, 0.0)
            za[line, 8:104, :] = z
            qa[line, 8:104, :] = kx * z
        else:
            db[line] = jnp.zeros((EXT, MODES), F32)

    def inner(ref, line, start):
        return ref[line, pl.ds(pl.multiple_of(start - 8, 8), CHUNK), :]

    buffers = ((za, qa), (zb, qb))
    for t in range(SWEEPS):
        (z_ref, q_ref), (z_to, q_to) = buffers[t % 2], buffers[(t + 1) % 2]
        ratio = (1.0 - omega[t]) * 4.0 / omega[t]

        def sweep(line, start, z, q, u, v, t=t, z_to=z_to, q_to=q_to, ratio=ratio):
            kx = inner(kb, line, start)
            new = ratio * z + inner(gb, line, start) * (kx * u + (v - 8.0 * q))
            here = pl.ds(pl.multiple_of(start, 8), CHUNK)
            if t == SWEEPS - 1:
                rounded = new.astype(BF16)
                s_all[line - 2, pl.ds(pl.multiple_of(start - 8, 16), CHUNK), :] = rounded
                new = rounded.astype(F32)
            z_to[line, here, :] = new
            q_to[line, here, :] = kx * new

        walk(z_ref, q_ref, 2, EXT + 2, 2, sweep)

    z_ref, q_ref = buffers[SWEEPS % 2]

    def image(line, start, z, q, u, v):
        value = inner(db, line, start) * z + 2.0 * q - 0.25 * (inner(kb, line, start) * u + v)
        i_all[line - 1, pl.ds(pl.multiple_of(start - 8, 16), CHUNK), :] = value.astype(BF16)

    walk(z_ref, q_ref, 1, EXT + 3, 2, image)

    total_self = jnp.zeros((MODES, MODES), F32)
    for a in range(0, EXT, 8):
        total_self += lax.dot_general(
            s_all[a : a + 8].reshape(8 * EXT, MODES),
            i_all[a + 1 : a + 9].reshape(8 * EXT, MODES),
            (((0,), (0,)), ((), ())),
            preferred_element_type=F32,
        )
    self_ref[...] = total_self.astype(BF16)

    row_s[...] = s_all[79:96]
    row_i[...] = i_all[0:17]
    col_s[:, 0:16, :] = s_all[:, 0:16, :]
    col_s[:, 16:32, :] = s_all[:, 80:96, :]
    col_i[:, 0:16, :] = i_all[0:98, 0:16, :]
    col_i[:, 16:32, :] = i_all[0:98, 80:96, :]

    def ring(column, lane):
        z, q = z_ref[:, column, :], q_ref[:, column, :]
        u = z[0:98] + z[2:100] + 2.0 * z[1:99]
        v = q[0:98] + q[2:100] + 2.0 * q[1:99]
        return -0.25 * (k[7:105, lane : lane + 1] * u + v)

    low, high = ring(8, 7), ring(103, 104)
    s_low, s_high = z_ref[2:98, 8 + 16, :], z_ref[2:98, 8 + 79, :]
    for n, part in enumerate((low[1:49], s_high[0:48], s_high[48:96], low[49:97])):
        edges[n] = part.astype(BF16)
    for n, part in enumerate(
        (low[0:9], s_high[79:88], s_high[88:96], low[9:17],
         high[0:9], s_low[79:88], s_low[88:96], high[9:17])
    ):
        filled = jnp.concatenate([part, jnp.zeros((16 - part.shape[0], MODES), F32)], axis=0)
        corners[n] = filled.astype(BF16)

    places = place_ref.shape[0]
    most = places // 8 // lax.axis_size("col")
    lane = lax.broadcasted_iota(jnp.int32, (places, MODES), 1)
    line = lax.broadcasted_iota(jnp.int32, (places, MODES), 0)
    slot = jnp.full((places, MODES), -1, jnp.int32)
    names = [owners_ref[0, g] for g in range(GROUPS)]
    for g in range(GROUPS):
        rank = jnp.int32(0)
        for earlier in range(g):
            rank = rank + (names[earlier] == names[g]).astype(jnp.int32)
        slot = jnp.where(lane // 8 == g, names[g] * most + rank, slot)
    found = (line // 8 == slot) & (line % 8 == lane % 8)
    place_ref[...] = found.astype(F32).astype(BF16)


def smooth(coefficients, modes, owners, places):
    shape = jax.ShapeDtypeStruct
    return pl.pallas_call(
        smooth_kernel,
        out_shape=(
            shape((17, EXT, MODES), BF16),
            shape((17, EXT, MODES), BF16),
            shape((EXT, 32, MODES), BF16),
            shape((EXT + 2, 32, MODES), BF16),
            shape((4, 48, MODES), BF16),
            shape((8, 16, MODES), BF16),
            shape((MODES, MODES), BF16),
            shape((places, MODES), BF16),
        ),
        in_specs=[VMEM, VMEM, SMEM],
        out_specs=(VMEM,) * 8,
        scratch_shapes=[pltpu.VMEM((EXT + 4, EXT, MODES), F32)] * 3
        + [pltpu.VMEM((EXT + 4, FRAME, MODES), F32)] * 4
        + [pltpu.VMEM((EXT, EXT, MODES), BF16), pltpu.VMEM((EXT + 2, EXT, MODES), BF16)],
        compiler_params=pltpu.CompilerParams(vmem_limit_bytes=60 * 2**20),
    )(coefficients, modes, owners)


def contract(first, second):
    return lax.dot_general(
        first.reshape(-1, MODES),
        second.reshape(-1, MODES),
        (((0,), (0,)), ((), ())),
        preferred_element_type=F32,
    )


def exchange_kernel(
    row_s, row_i, col_s, col_i, edges, corners, self_ref, place_ref, out_ref,
    row_2, row_1, col_2, col_1, cor_2, cor_1, edge_in, corner_in, partial_out, partial_in, outgoing,
    send, recv, psend, precv, asend, arecv,
):
    rows, cols = lax.axis_size("row"), lax.axis_size("col")
    r, c = lax.axis_index("row"), lax.axis_index("col")
    greet(
        [neighbour(a, b) for a, b in AROUND] + [neighbour(0, d) for d in range(1, cols)]
    )
    plan = []
    for n, (a, b) in enumerate(PAIRS):
        down, up = (-a, -b), (a, b)
        if n == 0:
            plan.append((down, row_i.at[0:9], row_2))
            plan.append((up, row_s.at[9:17], row_1))
        elif n == 1:
            plan.append((down, col_i.at[1:49, 0:16], col_2))
            plan.append((down, edges.at[0], edge_in.at[0]))
            plan.append((up, col_s.at[48:96, 16:32], col_1))
            plan.append((up, edges.at[2], edge_in.at[1]))
        else:
            m = n - 2
            image_cols = pl.ds(16 * m, 16)
            mode_cols = pl.ds(16 - 16 * m, 16)
            plan.append((down, col_i.at[0:9, image_cols], cor_2.at[m]))
            plan.append((down, corners.at[4 * m], corner_in.at[2 * m]))
            plan.append((up, col_s.at[88:96, mode_cols], cor_1.at[m]))
            plan.append((up, corners.at[4 * m + 2], corner_in.at[2 * m + 1]))
    copies = []
    for n, (to, src, dst) in enumerate(plan):
        copy = pltpu.make_async_remote_copy(
            src_ref=src,
            dst_ref=dst,
            send_sem=send.at[n],
            recv_sem=recv.at[n],
            device_id=neighbour(*to),
            device_id_type=MESH,
        )
        copy.start()
        copies.append(copy)

    place = place_ref[...]

    def put(slot, block, transposed):
        dims = (((1,), (1 if transposed else 0,)), ((), ()))
        rows_out = lax.dot_general(place, block, dims, preferred_element_type=F32)
        outgoing[:, slot] = rows_out.astype(BF16).reshape(cols, -1, MODES)

    put(0, self_ref[...], False)

    halves = []
    order = (2, 3, 0, 1)
    first_of = {0: 0, 1: 2, 2: 6, 3: 10}
    halves = {}
    pcopies = {}
    for n in order:
        base = first_of[n]
        a, b = PAIRS[n]
        if n == 0:
            copies[base].wait_recv()
            lower = contract(row_s[0:9], row_2[...])
            copies[base + 1].wait_recv()
            upper = contract(row_1[...], row_i[9:17])
        elif n == 1:
            copies[base].wait_recv()
            copies[base + 1].wait_recv()
            lower = contract(col_s[0:48, 16:32], col_2[...]) + contract(edges[1], edge_in[0])
            copies[base + 2].wait_recv()
            copies[base + 3].wait_recv()
            upper = contract(col_1[...], col_i[49:97, 0:16]) + contract(edge_in[1], edges[3])
        else:
            m = n - 2
            image_cols = slice(16 * m, 16 * m + 16)
            mode_cols = slice(16 - 16 * m, 32 - 16 * m)
            copies[base].wait_recv()
            copies[base + 1].wait_recv()
            lower = contract(col_s[79:88, mode_cols], cor_2[m]) + contract(
                corners[4 * m + 1], corner_in[2 * m]
            )
            copies[base + 2].wait_recv()
            copies[base + 3].wait_recv()
            upper = contract(cor_1[m], col_i[9:17, image_cols]) + contract(
                corner_in[2 * m + 1], corners[4 * m + 3]
            )
        partial_out[2 * n] = lower.astype(BF16)
        partial_out[2 * n + 1] = upper.astype(BF16)
        halves[n] = (lower, upper)
        for half, to in ((0, (a, b)), (1, (-a, -b))):
            copy = pltpu.make_async_remote_copy(
                src_ref=partial_out.at[2 * n + half],
                dst_ref=partial_in.at[2 * n + half],
                send_sem=psend.at[2 * n + half],
                recv_sem=precv.at[2 * n + half],
                device_id=neighbour(*to),
                device_id_type=MESH,
            )
            copy.start()
            pcopies[2 * n + half] = copy
    as_lower = {0: 7, 1: 5, 2: 8, 3: 6}
    as_upper = {0: 2, 1: 4, 2: 1, 3: 3}
    for n in order:
        a, b = PAIRS[n]
        lower, upper = halves[n]
        pcopies[2 * n + 1].wait_recv()
        valid = (r + a < rows) & (c + b >= 0) & (c + b < cols)
        block = lower + partial_in[2 * n + 1].astype(F32)
        put(as_lower[n], jnp.where(valid, block, 0.0).astype(BF16), False)
        pcopies[2 * n].wait_recv()
        valid = (r - a >= 0) & (c - b >= 0) & (c - b < cols)
        block = upper + partial_in[2 * n].astype(F32)
        put(as_upper[n], jnp.where(valid, block, 0.0).astype(BF16), True)
    for copy in copies:
        copy.wait_send()
    for copy in pcopies.values():
        copy.wait_send()

    out_ref[c] = outgoing[c]
    acopies = []
    for d in range(1, cols):
        to = neighbour(0, d)
        copy = pltpu.make_async_remote_copy(
            src_ref=outgoing.at[to[1]],
            dst_ref=out_ref.at[c],
            send_sem=asend.at[d],
            recv_sem=arecv.at[d],
            device_id=to,
            device_id_type=MESH,
        )
        copy.start()
        acopies.append(copy)
    for copy in acopies:
        copy.wait()


def exchange(parts, cols, places):
    per = places // cols
    shape = (cols, 9, per, MODES)
    dma = pltpu.SemaphoreType.DMA
    return pl.pallas_call(
        exchange_kernel,
        out_shape=jax.ShapeDtypeStruct(shape, BF16),
        in_specs=[VMEM] * 8,
        out_specs=VMEM,
        scratch_shapes=[
            pltpu.VMEM((9, EXT, MODES), BF16),
            pltpu.VMEM((8, EXT, MODES), BF16),
            pltpu.VMEM((48, 16, MODES), BF16),
            pltpu.VMEM((48, 16, MODES), BF16),
            pltpu.VMEM((2, 9, 16, MODES), BF16),
            pltpu.VMEM((2, 8, 16, MODES), BF16),
            pltpu.VMEM((2, 48, MODES), BF16),
            pltpu.VMEM((4, 16, MODES), BF16),
            pltpu.VMEM((8, MODES, MODES), BF16),
            pltpu.VMEM((8, MODES, MODES), BF16),
            pltpu.VMEM(shape, BF16),
            dma((14,)),
            dma((14,)),
            dma((8,)),
            dma((8,)),
            dma((cols,)),
            dma((cols,)),
        ],
        compiler_params=pltpu.CompilerParams(
            collective_id=1, has_side_effects=True, vmem_limit_bytes=40 * 2**20
        ),
    )(*parts)


def spread_kernel(got_ref, self_ref, cross_ref):
    most = got_ref.shape[2] // 8
    for source in range(got_ref.shape[0]):
        for rank in range(most):
            rows = slice(8 * rank, 8 * rank + 8)
            self_ref[0, source * most + rank] = got_ref[source, 0].astype(F32)[rows]
            for s in range(8):
                cross_ref[0, source * most + rank, s] = got_ref[source, 1 + s].astype(F32)[rows]


def spread(got, slots):
    return pl.pallas_call(
        spread_kernel,
        out_shape=(
            jax.ShapeDtypeStruct((1, slots, 8, MODES), F32),
            jax.ShapeDtypeStruct((1, slots, 8, 8, MODES), F32),
        ),
        in_specs=[VMEM],
        out_specs=(VMEM, VMEM),
    )(got)


def on_device(modes, conductivity, storage, owners, slots, cols):
    places = slots * 8
    coefficients = around(conductivity, storage)
    parts = smooth(coefficients, modes, owners.reshape(1, GROUPS), places)
    got = exchange(parts, cols, places)
    return spread(got, slots)


def solution(mesh):
    cols = mesh.shape["col"]
    return jax.shard_map(
        functools.partial(on_device, slots=2 * cols, cols=cols),
        mesh=mesh,
        in_specs=(
            P("row", "col", None),
            P("row", "col"),
            P("row", "col"),
            P("row", "col", None, None),
        ),
        out_specs=(P("row", "col", None, None), P("row", "col", None, None, None)),
        check_vma=False,
    )
```

```python
import functools
import math

import jax
import jax.numpy as jnp
from jax import lax
from jax.experimental import pallas as pl
from jax.experimental.pallas import tpu as pltpu
from jax.sharding import PartitionSpec as P

CELLS = 80
EXT = 96
MODES = 128
SWEEPS = 3
GROUPS = 16
FRAME = 112
CHUNK = 32
MESH = pl.DeviceIdType.MESH
F32 = jnp.float32
BF16 = jnp.bfloat16
VMEM = pl.BlockSpec(memory_space=pltpu.VMEM)
SMEM = pl.BlockSpec(memory_space=pltpu.SMEM)
BLOCKS = (22, 54, 86, 98)
UNROLL = 8


def neighbour(da, db):
    rows, cols = lax.axis_size("row"), lax.axis_size("col")
    r, c = lax.axis_index("row"), lax.axis_index("col")
    return (lax.rem(r + da + rows, rows), lax.rem(c + db + cols, cols))


AROUND = tuple((a, b) for a in (-1, 0, 1) for b in (-1, 0, 1) if (a, b) != (0, 0))


def omegas():
    return [
        1.0 / (1.15 + 0.85 * math.cos(math.pi * (2 * t + 1) / (2 * SWEEPS))) for t in range(SWEEPS)
    ]


def remote(src, dst, send, recv, to):
    return pltpu.make_async_remote_copy(
        src_ref=src, dst_ref=dst, send_sem=send, recv_sem=recv, device_id=to, device_id_type=MESH
    )


def lanes(shape):
    return lax.broadcasted_iota(jnp.int32, shape, 1)


def across(ref, line, start):
    low = ref[line, pl.ds(start - 1, CHUNK), :]
    mid = ref[line, pl.ds(pl.multiple_of(start, 8), CHUNK), :]
    high = ref[line, pl.ds(start + 1, CHUNK), :]
    return mid, (low + high) + (mid + mid)


def walk(z_ref, q_ref, first, last, body):
    @pl.loop(0, EXT // CHUNK)
    def _(chunk):
        start = 8 + chunk * CHUNK
        zc, hz = across(z_ref, first, start)
        qc, hq = across(q_ref, first, start)
        _, hz0 = across(z_ref, first - 1, start)
        _, hq0 = across(q_ref, first - 1, start)

        def step(line, carry):
            zc, hz, pz, qc, hq, pq = carry
            zn, hzn = across(z_ref, line + 1, start)
            qn, hqn = across(q_ref, line + 1, start)
            pzn, pqn = hz + hzn, hq + hqn
            body(line, start, zc, qc, pz + pzn, pq + pqn)
            return zn, hzn, pzn, qn, hqn, pqn

        lax.fori_loop(
            first, last, step, (zc, hz, hz0 + hz, qc, hq, hq0 + hq), unroll=UNROLL
        )


def contract(first, second):
    return lax.dot_general(
        first.reshape(-1, MODES),
        second.reshape(-1, MODES),
        (((0,), (0,)), ((), ())),
        preferred_element_type=F32,
    )


def padded(part, rows):
    return jnp.concatenate([part, jnp.zeros((rows - part.shape[0], MODES), F32)], axis=0)


def kernel(
    k_ref, s_ref, modes_hbm, owners_ref, out_ref,
    mid, side, left, right, modes_ref, kb, gb, db, za, qa, zb, qb, s_all, i_all,
    row_in, cor_in, col_i_in, col_s_in, ring_low, s_high, edge_i_in, edge_s_in,
    cor_ring, cor_ring_in, cor_own, partial_out, partial_in, outgoing,
    modes_sem, hsend, hrecv, send, recv, psend, precv, asend, arecv,
):
    rows, cols = lax.axis_size("row"), lax.axis_size("col")
    r, c = lax.axis_index("row"), lax.axis_index("col")
    fetch = pltpu.make_async_copy(modes_hbm, modes_ref, modes_sem)
    fetch.start()
    barrier = pltpu.get_barrier_semaphore()
    others = [neighbour(a, b) for a, b in AROUND] + [neighbour(0, d) for d in range(1, cols)]
    for device in others:
        pl.semaphore_signal(barrier, inc=1, device_id=device, device_id_type=MESH)

    k, s = [
        jnp.concatenate(
            [jnp.zeros((CELLS, 16), F32), ref[...], jnp.zeros((CELLS, 32), F32)], axis=1
        )
        for ref in (k_ref, s_ref)
    ]
    lane = lanes((CELLS, 128))
    mid[0, 16:96, :] = k
    mid[1, 16:96, :] = s
    packed = jnp.where(lane < 64, pltpu.roll(s, 96, 1), 0.0)
    packed = jnp.where(lane < 48, pltpu.roll(k, 80, 1), packed)
    packed = jnp.where(lane < 32, s, packed)
    packed = jnp.where(lane < 16, pltpu.roll(k, 112, 1), packed)
    side[...] = packed
    pl.semaphore_wait(barrier, len(others))
    halo = []
    for n, ((a, b), src, dst) in enumerate(
        (
            ((-1, 0), mid.at[:, 16:32, :], mid.at[:, 96:112, :]),
            ((1, 0), mid.at[:, 80:96, :], mid.at[:, 0:16, :]),
            ((0, -1), side, right.at[16:96, :]),
            ((0, 1), side, left.at[16:96, :]),
            ((-1, -1), side.at[0:16, :], right.at[96:112, :]),
            ((-1, 1), side.at[0:16, :], left.at[96:112, :]),
            ((1, -1), side.at[64:80, :], right.at[0:16, :]),
            ((1, 1), side.at[64:80, :], left.at[0:16, :]),
        )
    ):
        copy = remote(src, dst, hsend.at[n], hrecv.at[n], neighbour(a, b))
        copy.start()
        halo.append(copy)

    omega = omegas()
    scale = 1.0
    for w in omega:
        scale = scale * w / 4.0
    edge = jnp.zeros((8, MODES), F32)
    for ref in (za, qa, zb, qb):
        for line in (0, 1, EXT + 2, EXT + 3):
            ref[line] = jnp.zeros((FRAME, MODES), F32)

    @pl.loop(2, EXT + 2)
    def _(line):
        for ref in (za, qa, zb, qb):
            ref[line, 0:8, :] = edge
            ref[line, 104:112, :] = edge

    cell = lax.broadcasted_iota(jnp.int32, (EXT, MODES), 0)
    first_b, last_b = jnp.where(c == 0, 8, 0), jnp.where(c == cols - 1, 88, EXT)
    weight = jnp.where((cell >= first_b) & (cell < last_b), scale, 0.0)
    fetch.wait()

    def begin(line, carry):
        off = ((r == 0) & (line < 10)) | ((r == rows - 1) & (line >= 90))
        za[line, 8:104, :] = modes_ref[line - 2].astype(F32) * jnp.where(off, 0.0, weight)
        return carry

    lax.fori_loop(2, EXT + 2, begin, 0, unroll=4)

    places = cols * outgoing.shape[2]
    most = outgoing.shape[2] // 8
    lane = lax.broadcasted_iota(jnp.int32, (places, MODES), 1)
    line = lax.broadcasted_iota(jnp.int32, (places, MODES), 0)
    slot = jnp.full((places, MODES), -1, jnp.int32)
    names = [owners_ref[0, g] for g in range(GROUPS)]
    for g in range(GROUPS):
        rank = jnp.int32(0)
        for earlier in range(g):
            rank = rank + (names[earlier] == names[g]).astype(jnp.int32)
        slot = jnp.where(lane // 8 == g, names[g] * most + rank, slot)
    place = ((line // 8 == slot) & (line % 8 == lane % 8)).astype(F32).astype(BF16)

    for copy in halo:
        copy.wait()

    lane = lanes((FRAME, 128))
    line = lax.broadcasted_iota(jnp.int32, (FRAME, 128), 0)
    first_a, last_a = jnp.where(r == 0, 16, 0), jnp.where(r == rows - 1, 96, FRAME)
    first_b, last_b = jnp.where(c == 0, 16, 0), jnp.where(c == cols - 1, 96, FRAME)
    inside = (line >= first_a) & (line < last_a) & (lane >= first_b) & (lane < last_b)
    low, high = left[...], right[...]
    whole = []
    for n, (shift_low, shift_high) in enumerate(((96, 96), (80, 80))):
        x = jnp.where(lane < 96, mid[n], pltpu.roll(high, shift_high, 1))
        x = jnp.where(lane < 16, pltpu.roll(low, shift_low, 1), x)
        whole.append(jnp.where(inside, x, 0.0))
    k, s = whole
    inside = inside.astype(F32)

    def three(x, axis):
        return pltpu.roll(x, 1, axis) + pltpu.roll(x, 127, axis) + 2.0 * x

    total = three(three(padded(k, 128), 0), 1)[:FRAME]
    diagonal = s + 2.0 * k + 0.25 * total
    inverse = inside / (diagonal + (1.0 - inside))
    columns = [padded(x, 128).T[8 : 8 + EXT] for x in (k, inverse, diagonal)]
    for line in range(1, EXT + 3):
        at = line + 6
        kx = jnp.broadcast_to(columns[0][:, at : at + 1], (EXT, MODES))
        kb[line] = kx
        if 2 <= line < EXT + 2:
            gb[line] = jnp.broadcast_to(columns[1][:, at : at + 1], (EXT, MODES))
            db[line] = jnp.broadcast_to(columns[2][:, at : at + 1], (EXT, MODES))
            qa[line, 8:104, :] = kx * za[line, 8:104, :]
        else:
            db[line] = jnp.zeros((EXT, MODES), F32)

    def inner(ref, line, start):
        return ref[line, pl.ds(pl.multiple_of(start - 8, 8), CHUNK), :]

    buffers = ((za, qa), (zb, qb))

    def sweep(t):
        z_to, q_to = buffers[(t + 1) % 2]
        ratio = (1.0 - omega[t]) * 4.0 / omega[t]

        def body(line, start, z, q, u, v):
            kx = inner(kb, line, start)
            new = ratio * z + inner(gb, line, start) * (kx * u + (v - 8.0 * q))
            here = pl.ds(pl.multiple_of(start, 8), CHUNK)
            if t == SWEEPS - 1:
                rounded = new.astype(BF16)
                s_all[line - 2, pl.ds(pl.multiple_of(start - 8, 16), CHUNK), :] = rounded
                new = rounded.astype(F32)
            z_to[line, here, :] = new
            q_to[line, here, :] = kx * new

        return body

    def image(line, start, z, q, u, v):
        value = inner(db, line, start) * z + 2.0 * q - 0.25 * (inner(kb, line, start) * u + v)
        i_all[line - 1, pl.ds(pl.multiple_of(start - 8, 16), CHUNK), :] = value.astype(BF16)

    z_ref, q_ref = buffers[SWEEPS % 2]

    def ring(column, lane, first, last):
        n = last - first
        z = z_ref[first - 1 : last + 1, column, :]
        q = q_ref[first - 1 : last + 1, column, :]
        u = z[0:n] + z[2 : n + 2] + 2.0 * z[1 : n + 1]
        v = q[0:n] + q[2 : n + 2] + 2.0 * q[1 : n + 1]
        return -0.25 * (k[first + 6 : last + 6, lane : lane + 1] * u + v)

    copies = []

    def ship(to, src, dst):
        n = len(copies)
        copy = remote(src, dst, send.at[n], recv.at[n], neighbour(*to))
        copy.start()
        copies.append(copy)

    def ship_columns(image_lines, mode_lines, image_edge, mode_edge, at, edge_at):
        count = image_lines[1] - image_lines[0]
        ship((0, -1), i_all.at[image_lines[0] + 1 : image_lines[1] + 1, 0:16],
             col_i_in.at[at : at + count])
        ship((0, -1), ring_low.at[image_edge : image_edge + 16],
             edge_i_in.at[edge_at : edge_at + 16])
        ship((0, 1), s_all.at[mode_lines[0] : mode_lines[1], 80:96],
             col_s_in.at[at : at + count])
        ship((0, 1), s_high.at[mode_edge : mode_edge + 16],
             edge_s_in.at[edge_at : edge_at + 16])

    done = 0
    start = [2] * SWEEPS + [1]
    for n, stop in enumerate(BLOCKS):
        final = n == len(BLOCKS) - 1
        for t in range(SWEEPS):
            end = stop if final else stop - t
            walk(*buffers[t % 2], start[t], end, sweep(t))
            start[t] = end
        end = EXT + 3 if final else stop - SWEEPS
        walk(z_ref, q_ref, start[SWEEPS], end, image)
        start[SWEEPS] = end
        ready = EXT if final else (end - 2) // 16 * 16
        ring_low[done:ready, :] = ring(8, 7, done + 2, ready + 2).astype(BF16)
        s_high[done:ready, :] = z_ref[done + 2 : ready + 2, 8 + 79, :].astype(BF16)
        done = ready
        if n == 0:
            cor_ring[0] = padded(ring(8, 7, 1, 18), 32).astype(BF16)
            cor_ring[1] = padded(ring(103, 104, 1, 18), 32).astype(BF16)
            ship_columns((0, 8), (8, 16), 0, 0, 0, 0)
            ship((-1, 0), i_all.at[0:17], row_in)
            ship((-1, -1), i_all.at[0:17, 0:16], cor_in.at[0])
            ship((-1, -1), cor_ring.at[0], cor_ring_in.at[0])
            ship((-1, 1), i_all.at[0:17, 80:96], cor_in.at[1])
            ship((-1, 1), cor_ring.at[1], cor_ring_in.at[1])
        elif n == 1:
            ship_columns((16, 32), (32, 48), 16, 32, 8, 16)
        elif n == 2:
            ship_columns((48, 64), (64, 80), 48, 64, 24, 32)
        else:
            ship_columns((80, 96), (80, 96), 80, 80, 40, 48)

    returned = {}

    def give(n, block, to):
        partial_out[n] = block.astype(BF16)
        copy = remote(partial_out.at[n], partial_in.at[n], psend.at[n], precv.at[n], neighbour(*to))
        copy.start()
        returned[n] = copy

    half = lax.broadcasted_iota(jnp.int32, (16, MODES), 0) < 8

    def some(ref, first):
        x = ref[0:16].astype(F32)
        return (jnp.where(half, x, 0.0) if first else jnp.where(half, 0.0, x)).astype(BF16)

    for copy in copies[0:4] + copies[9:17]:
        copy.wait_recv()
    col_lower = contract(s_all[0:8, 80:96], col_i_in[0:8])
    col_lower += contract(s_all[16:32, 80:96], col_i_in[8:24])
    col_lower += contract(s_all[48:64, 80:96], col_i_in[24:40])
    col_lower += contract(some(s_high, True), edge_i_in[0:16])
    col_lower += contract(s_high[16:32], edge_i_in[16:32])
    col_lower += contract(s_high[48:64], edge_i_in[32:48])
    give(0, col_lower, (0, 1))
    col_upper = contract(col_s_in[0:8], i_all[9:17, 0:16])
    col_upper += contract(col_s_in[8:24], i_all[33:49, 0:16])
    col_upper += contract(col_s_in[24:40], i_all[65:81, 0:16])
    col_upper += contract(edge_s_in[0:16], some(ring_low, False))
    col_upper += contract(edge_s_in[16:32], ring_low[32:48])
    col_upper += contract(edge_s_in[32:48], ring_low[64:80])
    give(1, col_upper, (0, -1))
    cor_own[0] = padded(z_ref[81:98, 8 + 79, :], 32).astype(BF16)
    cor_own[1] = padded(z_ref[81:98, 8 + 16, :], 32).astype(BF16)
    for copy in copies[4:9]:
        copy.wait_recv()
    ahead = contract(s_all[79:96, 80:96], cor_in[0]) + contract(cor_own[0], cor_ring_in[0])
    give(2, ahead, (1, 1))
    behind = contract(s_all[79:96, 0:16], cor_in[1]) + contract(cor_own[1], cor_ring_in[1])
    give(3, behind, (1, -1))
    below = contract(s_all[79:96], row_in[...])
    give(4, below, (1, 0))

    def put(slot, block, transposed=False):
        dims = (((1,), (1 if transposed else 0,)), ((), ()))
        rows_out = lax.dot_general(place, block, dims, preferred_element_type=F32)
        outgoing[:, slot] = rows_out.astype(BF16).reshape(cols, -1, MODES)

    def where(a, b, block):
        valid = (r + a >= 0) & (r + a < rows) & (c + b >= 0) & (c + b < cols)
        return jnp.where(valid, block, 0.0).astype(BF16)

    acopies = []

    def scatter(part, first, last):
        out_ref[c, first:last] = outgoing[c, first:last]
        for d in range(1, cols):
            to = neighbour(0, d)
            copy = remote(
                outgoing.at[to[1], first:last],
                out_ref.at[c, first:last],
                asend.at[part, d],
                arecv.at[part, d],
                to,
            )
            copy.start()
            acopies.append(copy)

    total_self = jnp.zeros((MODES, MODES), F32)
    for a in range(0, EXT, 8):
        total_self += contract(s_all[a : a + 8], i_all[a + 1 : a + 9])
    put(0, total_self.astype(BF16))
    put(1, where(1, -1, behind))
    put(2, where(1, 0, below))
    put(3, where(1, 1, ahead))
    scatter(0, 0, 4)
    for copy in copies[17:21]:
        copy.wait_recv()
    late_lower = contract(s_all[80:96, 80:96], col_i_in[40:56])
    late_lower += contract(s_high[80:96], edge_i_in[48:64])
    late_upper = contract(col_s_in[40:56], i_all[81:97, 0:16])
    late_upper += contract(edge_s_in[48:64], ring_low[80:96])
    returned[1].wait_recv()
    put(4, where(0, 1, col_lower + late_lower + partial_in[1].astype(F32)))
    returned[0].wait_recv()
    put(5, where(0, -1, col_upper + late_upper + partial_in[0].astype(F32)), True)
    for n, slot, (a, b) in ((2, 6, (-1, -1)), (3, 8, (-1, 1)), (4, 7, (-1, 0))):
        returned[n].wait_recv()
        put(slot, where(a, b, partial_in[n].astype(F32)), True)
    scatter(1, 4, 9)
    for copy in copies:
        copy.wait_send()
    for copy in returned.values():
        copy.wait_send()
    for copy in acopies:
        copy.wait()


ORDER = (None, 5, 6, 7, 4, 3, 0, 1, 2)


def assemble(conductivity, storage, modes, owners, cols, slots):
    shape = (cols, 9, slots // cols * 8, MODES)
    dma = pltpu.SemaphoreType.DMA

    def bf(*dims):
        return pltpu.VMEM(dims, BF16)

    def f(*dims):
        return pltpu.VMEM(dims, F32)

    return pl.pallas_call(
        kernel,
        out_shape=jax.ShapeDtypeStruct(shape, BF16),
        in_specs=[VMEM, VMEM, pl.BlockSpec(memory_space=pl.ANY), SMEM],
        out_specs=VMEM,
        scratch_shapes=[
            f(2, FRAME, 128), f(CELLS, 128), f(FRAME, 128), f(FRAME, 128), bf(EXT, EXT, MODES),
            *[f(EXT + 4, EXT, MODES)] * 3,
            *[f(EXT + 4, FRAME, MODES)] * 4,
            bf(EXT, EXT, MODES), bf(EXT + 2, EXT, MODES),
            bf(17, EXT, MODES), bf(2, 17, 16, MODES), bf(56, 16, MODES), bf(56, 16, MODES),
            bf(EXT, MODES), bf(EXT, MODES), bf(64, MODES), bf(64, MODES),
            bf(2, 32, MODES), bf(2, 32, MODES), bf(2, 32, MODES),
            bf(5, MODES, MODES), bf(5, MODES, MODES), bf(*shape),
            dma, dma((8,)), dma((8,)), dma((21,)), dma((21,)), dma((5,)), dma((5,)),
            dma((2, cols)), dma((2, cols)),
        ],
        compiler_params=pltpu.CompilerParams(
            collective_id=0, has_side_effects=True, vmem_limit_bytes=60 * 2**20
        ),
    )(conductivity, storage, modes, owners)


def spread_kernel(got_ref, self_ref, cross_ref):
    most = got_ref.shape[2] // 8
    for source in range(got_ref.shape[0]):
        for slot, s in enumerate(ORDER):
            x = got_ref[source, slot].astype(F32)
            for rank in range(most):
                part = x[8 * rank : 8 * rank + 8]
                if s is None:
                    self_ref[0, source * most + rank] = part
                else:
                    cross_ref[0, source * most + rank, s] = part


def spread(got, slots):
    return pl.pallas_call(
        spread_kernel,
        out_shape=(
            jax.ShapeDtypeStruct((1, slots, 8, MODES), F32),
            jax.ShapeDtypeStruct((1, slots, 8, 8, MODES), F32),
        ),
        in_specs=[VMEM],
        out_specs=(VMEM, VMEM),
    )(got)


def on_device(modes, conductivity, storage, owners, slots, cols):
    got = assemble(conductivity, storage, modes, owners.reshape(1, GROUPS), cols, slots)
    return spread(got, slots)


def solution(mesh):
    cols = mesh.shape["col"]
    return jax.shard_map(
        functools.partial(on_device, slots=2 * cols, cols=cols),
        mesh=mesh,
        in_specs=(
            P("row", "col", None),
            P("row", "col"),
            P("row", "col"),
            P("row", "col", None, None),
        ),
        out_specs=(P("row", "col", None, None), P("row", "col", None, None, None)),
        check_vma=False,
    )
```

```python
import functools
import math

import jax
import jax.numpy as jnp
from jax import lax
from jax.experimental import pallas as pl
from jax.experimental.pallas import tpu as pltpu
from jax.sharding import PartitionSpec as P

CELLS = 80
EXT = 96
MODES = 128
SWEEPS = 3
GROUPS = 16
FRAME = 112
CHUNK = 48
MESH = pl.DeviceIdType.MESH
F32 = jnp.float32
BF16 = jnp.bfloat16
VMEM = pl.BlockSpec(memory_space=pltpu.VMEM)
SMEM = pl.BlockSpec(memory_space=pltpu.SMEM)
BLOCKS = (
    ((2, 22), (2, 21), (2, 20), (1, 19)),
    ((79, 98), (80, 98), (81, 98), (82, 99)),
    ((22, 46), (21, 45), (20, 44), (19, 43)),
    ((46, 70), (45, 69), (44, 68), (43, 67)),
    ((70, 79), (69, 80), (68, 81), (67, 82)),
)
SPREAD = ((1, 23), (78, 99), (23, 47), (47, 71), (71, 78))
EDGES = ((0, 16), (80, 96), (16, 32), (32, 64), (64, 80))
UNROLL = 12
PLANE = 4


def neighbour(da, db):
    rows, cols = lax.axis_size("row"), lax.axis_size("col")
    r, c = lax.axis_index("row"), lax.axis_index("col")
    return (lax.rem(r + da + rows, rows), lax.rem(c + db + cols, cols))


AROUND = tuple((a, b) for a in (-1, 0, 1) for b in (-1, 0, 1) if (a, b) != (0, 0))


def omegas():
    return [
        1.0 / (1.15 + 0.85 * math.cos(math.pi * (2 * t + 1) / (2 * SWEEPS))) for t in range(SWEEPS)
    ]


def remote(src, dst, send, recv, to):
    return pltpu.make_async_remote_copy(
        src_ref=src, dst_ref=dst, send_sem=send, recv_sem=recv, device_id=to, device_id_type=MESH
    )


def lanes(shape):
    return lax.broadcasted_iota(jnp.int32, shape, 1)


def across(ref, line, start):
    low = ref[line, pl.ds(start - 1, CHUNK), :]
    mid = ref[line, pl.ds(pl.multiple_of(start, 8), CHUNK), :]
    high = ref[line, pl.ds(start + 1, CHUNK), :]
    return mid, (low + high) + (mid + mid)


def walk(z_ref, q_ref, first, last, body):
    @pl.loop(0, EXT // CHUNK)
    def _(chunk):
        start = 8 + chunk * CHUNK
        zc, hz = across(z_ref, first, start)
        qc, hq = across(q_ref, first, start)
        _, hz0 = across(z_ref, first - 1, start)
        _, hq0 = across(q_ref, first - 1, start)

        def step(line, carry):
            zc, hz, pz, qc, hq, pq = carry
            zn, hzn = across(z_ref, line + 1, start)
            qn, hqn = across(q_ref, line + 1, start)
            pzn, pqn = hz + hzn, hq + hqn
            body(line, start, zc, qc, pz + pzn, pq + pqn)
            return zn, hzn, pzn, qn, hqn, pqn

        lax.fori_loop(
            first, last, step, (zc, hz, hz0 + hz, qc, hq, hq0 + hq), unroll=UNROLL
        )


def contract(first, second):
    return lax.dot_general(
        first.reshape(-1, MODES),
        second.reshape(-1, MODES),
        (((0,), (0,)), ((), ())),
        preferred_element_type=F32,
    )


def padded(part, rows):
    return jnp.concatenate([part, jnp.zeros((rows - part.shape[0], MODES), F32)], axis=0)


def kernel(
    k_ref, s_ref, modes_hbm, owners_ref, out_ref,
    mid, side, left, right, modes_ref, kb, gb, db, za, qa, zb, qb, s_all, i_all,
    row_in, cor_in, col_i_in, col_s_in, ring_low, s_high, edge_i_in, edge_s_in,
    cor_ring, cor_ring_in, cor_own, partial_out, partial_in, outgoing, relay,
    modes_sem, hsend, hrecv, send, recv, psend, precv, asend, arecv, csend, crecv, rrecv, fsend,
):
    rows, cols = lax.axis_size("row"), lax.axis_size("col")
    r, c = lax.axis_index("row"), lax.axis_index("col")
    fetch = pltpu.make_async_copy(modes_hbm, modes_ref, modes_sem)
    fetch.start()
    barrier = pltpu.get_barrier_semaphore()
    others = [neighbour(a, b) for a, b in AROUND] + [neighbour(0, d) for d in range(1, cols)]
    for device in others:
        pl.semaphore_signal(barrier, inc=1, device_id=device, device_id_type=MESH)

    k, s = [
        jnp.concatenate(
            [jnp.zeros((CELLS, 16), F32), ref[...], jnp.zeros((CELLS, 32), F32)], axis=1
        )
        for ref in (k_ref, s_ref)
    ]
    lane = lanes((CELLS, 128))
    mid[0, 16:96, :] = k
    mid[1, 16:96, :] = s
    packed = jnp.where(lane < 64, pltpu.roll(s, 96, 1), 0.0)
    packed = jnp.where(lane < 48, pltpu.roll(k, 80, 1), packed)
    packed = jnp.where(lane < 32, s, packed)
    packed = jnp.where(lane < 16, pltpu.roll(k, 112, 1), packed)
    side[...] = packed
    pl.semaphore_wait(barrier, len(others))
    halo = []
    for n, ((a, b), src, dst) in enumerate(
        (
            ((-1, 0), mid.at[:, 16:32, :], mid.at[:, 96:112, :]),
            ((1, 0), mid.at[:, 80:96, :], mid.at[:, 0:16, :]),
            ((0, -1), side, right.at[16:96, :]),
            ((0, 1), side, left.at[16:96, :]),
            ((-1, -1), side.at[0:16, :], right.at[96:112, :]),
            ((-1, 1), side.at[0:16, :], left.at[96:112, :]),
            ((1, -1), side.at[64:80, :], right.at[0:16, :]),
            ((1, 1), side.at[64:80, :], left.at[0:16, :]),
        )
    ):
        copy = remote(src, dst, hsend.at[n], hrecv.at[n], neighbour(a, b))
        copy.start()
        halo.append(copy)

    omega = omegas()
    scale = 1.0
    for w in omega:
        scale = scale * w / 4.0
    edge = jnp.zeros((8, MODES), F32)
    for ref in (za, qa, zb, qb):
        for line in (0, 1, EXT + 2, EXT + 3):
            ref[line] = jnp.zeros((FRAME, MODES), F32)

    @pl.loop(2, EXT + 2)
    def _(line):
        for ref in (za, qa, zb, qb):
            ref[line, 0:8, :] = edge
            ref[line, 104:112, :] = edge

    cell = lax.broadcasted_iota(jnp.int32, (EXT, MODES), 0)
    first_b, last_b = jnp.where(c == 0, 8, 0), jnp.where(c == cols - 1, 88, EXT)
    weight = jnp.where((cell >= first_b) & (cell < last_b), scale, 0.0)
    fetch.wait()

    def begin(line, carry):
        off = ((r == 0) & (line < 10)) | ((r == rows - 1) & (line >= 90))
        za[line, 8:104, :] = modes_ref[line - 2].astype(F32) * jnp.where(off, 0.0, weight)
        return carry

    lax.fori_loop(2, EXT + 2, begin, 0, unroll=4)

    places = cols * outgoing.shape[2]
    most = outgoing.shape[2] // 8
    lane = lax.broadcasted_iota(jnp.int32, (places, MODES), 1)
    line = lax.broadcasted_iota(jnp.int32, (places, MODES), 0)
    slot = jnp.full((places, MODES), -1, jnp.int32)
    names = [owners_ref[0, g] for g in range(GROUPS)]
    for g in range(GROUPS):
        rank = jnp.int32(0)
        for earlier in range(g):
            rank = rank + (names[earlier] == names[g]).astype(jnp.int32)
        slot = jnp.where(lane // 8 == g, names[g] * most + rank, slot)
    place = ((line // 8 == slot) & (line % 8 == lane % 8)).astype(F32).astype(BF16)

    for copy in halo:
        copy.wait()

    lane = lanes((FRAME, 128))
    line = lax.broadcasted_iota(jnp.int32, (FRAME, 128), 0)
    first_a, last_a = jnp.where(r == 0, 16, 0), jnp.where(r == rows - 1, 96, FRAME)
    first_b, last_b = jnp.where(c == 0, 16, 0), jnp.where(c == cols - 1, 96, FRAME)
    inside = (line >= first_a) & (line < last_a) & (lane >= first_b) & (lane < last_b)
    low, high = left[...], right[...]
    whole = []
    for n, (shift_low, shift_high) in enumerate(((96, 96), (80, 80))):
        x = jnp.where(lane < 96, mid[n], pltpu.roll(high, shift_high, 1))
        x = jnp.where(lane < 16, pltpu.roll(low, shift_low, 1), x)
        whole.append(jnp.where(inside, x, 0.0))
    k, s = whole
    inside = inside.astype(F32)

    def three(x, axis):
        return pltpu.roll(x, 1, axis) + pltpu.roll(x, 127, axis) + 2.0 * x

    total = three(three(padded(k, 128), 0), 1)[:FRAME]
    diagonal = s + 2.0 * k + 0.25 * total
    inverse = inside / (diagonal + (1.0 - inside))
    columns = [padded(x, 128).T[8 : 8 + EXT] for x in (k, inverse, diagonal)]
    def spread_lines(first, last):
        for line in range(first, last):
            at = line + 6
            kx = jnp.broadcast_to(columns[0][:, at : at + 1], (EXT, MODES))
            kb[line] = kx
            if 2 <= line < EXT + 2:
                gb[line] = jnp.broadcast_to(columns[1][:, at : at + 1], (EXT, MODES))
                db[line] = jnp.broadcast_to(columns[2][:, at : at + 1], (EXT, MODES))
                qa[line, 8:104, :] = kx * za[line, 8:104, :]
            else:
                db[line] = jnp.zeros((EXT, MODES), F32)

    def inner(ref, line, start):
        return ref[line, pl.ds(pl.multiple_of(start - 8, 8), CHUNK), :]

    buffers = ((za, qa), (zb, qb))

    def sweep(t):
        z_to, q_to = buffers[(t + 1) % 2]
        ratio = (1.0 - omega[t]) * 4.0 / omega[t]

        def body(line, start, z, q, u, v):
            kx = inner(kb, line, start)
            new = ratio * z + inner(gb, line, start) * (kx * u + (v - 8.0 * q))
            here = pl.ds(pl.multiple_of(start, 8), CHUNK)
            if t == SWEEPS - 1:
                rounded = new.astype(BF16)
                s_all[line - 2, pl.ds(pl.multiple_of(start - 8, 16), CHUNK), :] = rounded
                new = rounded.astype(F32)
            z_to[line, here, :] = new
            q_to[line, here, :] = kx * new

        return body

    def image(line, start, z, q, u, v):
        value = inner(db, line, start) * z + 2.0 * q - 0.25 * (inner(kb, line, start) * u + v)
        i_all[line - 1, pl.ds(pl.multiple_of(start - 8, 16), CHUNK), :] = value.astype(BF16)

    z_ref, q_ref = buffers[SWEEPS % 2]

    def ring(column, lane, first, last):
        n = last - first
        z = z_ref[first - 1 : last + 1, column, :]
        q = q_ref[first - 1 : last + 1, column, :]
        u = z[0:n] + z[2 : n + 2] + 2.0 * z[1 : n + 1]
        v = q[0:n] + q[2 : n + 2] + 2.0 * q[1 : n + 1]
        return -0.25 * (k[first + 6 : last + 6, lane : lane + 1] * u + v)

    copies = []

    def ship(to, src, dst):
        n = len(copies)
        copy = remote(src, dst, send.at[n], recv.at[n], neighbour(*to))
        copy.start()
        copies.append(copy)

    def ship_edges(at, image_edge, mode_edge):
        ship((0, -1), ring_low.at[image_edge : image_edge + 16], edge_i_in.at[at : at + 16])
        ship((0, 1), s_high.at[mode_edge : mode_edge + 16], edge_s_in.at[at : at + 16])

    x = lax.rem(c, PLANE)
    ways = (
        (i_all, lambda lines: (lines[0] + 1, 0), col_i_in, -1, 0, PLANE - 1),
        (s_all, lambda lines: (lines[0], 80), col_s_in, 1, PLANE - 1, 0),
    )
    pieces = (
        (((0, 8), (8, 16)), 0),
        (((80, 88), (88, 96)), 8),
        (((16, 24), (24, 32)), 16),
    )

    def strip(n, w, quarter=None, to=None):
        source, place_of, target, sign, _, _ = ways[w]
        lines, at = pieces[n]
        first, column = place_of(lines[w])
        count = lines[w][1] - lines[w][0]
        if quarter is None:
            quarter, size = 0, count
        else:
            size = count // PLANE
        src = source.at[pl.ds(first + quarter * size, size), column : column + 16]
        if to is None:
            return remote(src, target.at[pl.ds(at + quarter * size, size)], csend.at[n, w, quarter],
                          crecv.at[n, w, quarter], neighbour(0, sign))
        return remote(src, relay.at[n, w, 0:size], csend.at[n, w, quarter], rrecv.at[n, w],
                      neighbour(0, to))

    def onward(n, w):
        _, _, target, sign, _, _ = ways[w]
        lines, at = pieces[n]
        size = (lines[w][1] - lines[w][0]) // PLANE
        quarter = x if sign < 0 else PLANE - 1 - x
        return remote(relay.at[n, w, 0:size], target.at[pl.ds(at + quarter * size, size)],
                      fsend.at[n, w], crecv.at[n, w, quarter],
                      neighbour(0, sign * (1 + quarter)))

    def ship_columns(n):
        for w, (_, _, _, sign, sender, _) in enumerate(ways):

            @pl.when(x != sender)
            def _(n=n, w=w):
                strip(n, w).start()

            @pl.when(x == sender)
            def _(n=n, w=w, sign=sign):
                strip(n, w, 0).start()
                for q in range(1, PLANE):
                    strip(n, w, q, -sign * q).start()

    def pass_on(n):
        for w, (_, _, _, _, sender, _) in enumerate(ways):

            @pl.when(x != sender)
            def _(n=n, w=w):
                strip(n, w, 0, 1).wait_recv()
                onward(n, w).start()

    def columns_arrived(n):
        for w, (_, _, _, _, _, receiver) in enumerate(ways):

            @pl.when(x != receiver)
            def _(n=n, w=w):
                strip(n, w).wait_recv()

            @pl.when(x == receiver)
            def _(n=n, w=w):
                for q in range(PLANE):
                    strip(n, w, q).wait_recv()

    def columns_left(n):
        for w, (_, _, _, _, sender, _) in enumerate(ways):

            @pl.when(x != sender)
            def _(n=n, w=w):
                strip(n, w).wait_send()
                onward(n, w).wait_send()

            @pl.when(x == sender)
            def _(n=n, w=w):
                for q in range(PLANE):
                    strip(n, w, q).wait_send()

    returned = {}

    def give(n, block, to):
        partial_out[n] = block.astype(BF16)
        copy = remote(partial_out.at[n], partial_in.at[n], psend.at[n], precv.at[n], neighbour(*to))
        copy.start()
        returned[n] = copy

    def put(slot, block, transposed=False):
        dims = (((1,), (1 if transposed else 0,)), ((), ()))
        rows_out = lax.dot_general(place, block, dims, preferred_element_type=F32)
        outgoing[:, slot] = rows_out.astype(BF16).reshape(cols, -1, MODES)

    def where(a, b, block):
        valid = (r + a >= 0) & (r + a < rows) & (c + b >= 0) & (c + b < cols)
        return jnp.where(valid, block, 0.0).astype(BF16)

    acopies = []

    def scatter(part, first, last):
        out_ref[c, first:last] = outgoing[c, first:last]
        for d in range(1, cols):
            to = neighbour(0, d)
            copy = remote(
                outgoing.at[to[1], first:last],
                out_ref.at[c, first:last],
                asend.at[part, d],
                arecv.at[part, d],
                to,
            )
            copy.start()
            acopies.append(copy)

    for n, (block, (spread_first, spread_last), (edge_first, edge_last)) in enumerate(
        zip(BLOCKS, SPREAD, EDGES, strict=True)
    ):
        spread_lines(spread_first, spread_last)
        for t in range(SWEEPS):
            walk(*buffers[t % 2], *block[t], sweep(t))
        walk(z_ref, q_ref, *block[SWEEPS], image)
        first, last = edge_first + 2, edge_last + 2
        ring_low[edge_first:edge_last, :] = ring(8, 7, first, last).astype(BF16)
        s_high[edge_first:edge_last, :] = z_ref[first:last, 8 + 79, :].astype(BF16)
        if n == 0:
            cor_ring[0] = padded(ring(8, 7, 1, 18), 32).astype(BF16)
            cor_ring[1] = padded(ring(103, 104, 1, 18), 32).astype(BF16)
            ship((-1, 0), i_all.at[0:17], row_in)
            ship((-1, -1), i_all.at[0:17, 0:16], cor_in.at[0])
            ship((-1, -1), cor_ring.at[0], cor_ring_in.at[0])
            ship((-1, 1), i_all.at[0:17, 80:96], cor_in.at[1])
            ship((-1, 1), cor_ring.at[1], cor_ring_in.at[1])
            ship_columns(0)
            ship_edges(0, 0, 0)
        elif n == 1:
            ship_columns(1)
            ship_edges(16, 80, 80)
            pass_on(0)
            cor_own[0] = padded(z_ref[81:98, 8 + 79, :], 32).astype(BF16)
            cor_own[1] = padded(z_ref[81:98, 8 + 16, :], 32).astype(BF16)
        elif n == 2:
            ship_columns(2)
            ship_edges(32, 16, 16)
            pass_on(1)
        elif n == 3:
            ship((0, -1), i_all.at[33:49, 0:16], col_i_in.at[24:40])
            ship((0, 1), s_all.at[48:64, 80:96], col_s_in.at[24:40])
            ship_edges(48, 32, 48)
            pass_on(2)
        else:
            ship((0, -1), i_all.at[65:81, 0:16], col_i_in.at[40:56])
            ship((0, 1), s_all.at[64:80, 80:96], col_s_in.at[40:56])
            ship_edges(64, 64, 64)
            for copy in copies[0:5]:
                copy.wait_recv()
            ahead = contract(s_all[79:96, 80:96], cor_in[0])
            ahead += contract(cor_own[0], cor_ring_in[0])
            give(2, ahead, (1, 1))
            behind = contract(s_all[79:96, 0:16], cor_in[1])
            behind += contract(cor_own[1], cor_ring_in[1])
            give(3, behind, (1, -1))
            below = contract(s_all[79:96], row_in[...])
            give(4, below, (1, 0))
            put(0, where(1, -1, behind))
            put(1, where(1, 0, below))
            put(2, where(1, 1, ahead))

    half = lax.broadcasted_iota(jnp.int32, (16, MODES), 0) < 8

    def some(part, first):
        x = part.astype(F32)
        return (jnp.where(half, x, 0.0) if first else jnp.where(half, 0.0, x)).astype(BF16)

    for n in range(3):
        columns_arrived(n)
    for copy in copies[5:15]:
        copy.wait_recv()
    col_lower = contract(s_all[0:8, 80:96], col_i_in[0:8])
    col_lower += contract(s_all[80:88, 80:96], col_i_in[8:16])
    col_lower += contract(s_all[16:24, 80:96], col_i_in[16:24])
    col_lower += contract(s_all[32:48, 80:96], col_i_in[24:40])
    col_lower += contract(some(s_high[0:16], True), edge_i_in[0:16])
    col_lower += contract(some(s_high[80:96], True), edge_i_in[16:32])
    col_lower += contract(some(s_high[16:32], True), edge_i_in[32:48])
    col_lower += contract(s_high[32:48], edge_i_in[48:64])
    give(0, col_lower, (0, 1))
    col_upper = contract(col_s_in[0:8], i_all[9:17, 0:16])
    col_upper += contract(col_s_in[8:16], i_all[89:97, 0:16])
    col_upper += contract(col_s_in[16:24], i_all[25:33, 0:16])
    col_upper += contract(col_s_in[24:40], i_all[49:65, 0:16])
    col_upper += contract(edge_s_in[0:16], some(ring_low[0:16], False))
    col_upper += contract(edge_s_in[16:32], some(ring_low[80:96], False))
    col_upper += contract(edge_s_in[32:48], some(ring_low[16:32], False))
    col_upper += contract(edge_s_in[48:64], ring_low[48:64])
    give(1, col_upper, (0, -1))
    scatter(0, 0, 3)
    for n, slot, (a, b) in ((2, 4, (-1, -1)), (4, 5, (-1, 0)), (3, 6, (-1, 1))):
        returned[n].wait_recv()
        put(slot, where(a, b, partial_in[n].astype(F32)), True)
    total_self = jnp.zeros((MODES, MODES), F32)
    for a in range(0, EXT, 8):
        total_self += contract(s_all[a : a + 8], i_all[a + 1 : a + 9])
    put(3, total_self.astype(BF16))
    scatter(1, 3, 7)
    for copy in copies[15:19]:
        copy.wait_recv()
    late_lower = contract(s_all[64:80, 80:96], col_i_in[40:56])
    late_lower += contract(s_high[64:80], edge_i_in[64:80])
    late_upper = contract(col_s_in[40:56], i_all[65:81, 0:16])
    late_upper += contract(edge_s_in[64:80], ring_low[64:80])
    returned[1].wait_recv()
    put(7, where(0, 1, col_lower + late_lower + partial_in[1].astype(F32)))
    returned[0].wait_recv()
    put(8, where(0, -1, col_upper + late_upper + partial_in[0].astype(F32)), True)
    scatter(2, 7, 9)
    for n in range(3):
        columns_left(n)
    for copy in copies:
        copy.wait_send()
    for copy in returned.values():
        copy.wait_send()
    for copy in acopies:
        copy.wait()


ORDER = (5, 6, 7, None, 0, 1, 2, 4, 3)


def assemble(conductivity, storage, modes, owners, cols, slots):
    shape = (cols, 9, slots // cols * 8, MODES)
    dma = pltpu.SemaphoreType.DMA

    def bf(*dims):
        return pltpu.VMEM(dims, BF16)

    def f(*dims):
        return pltpu.VMEM(dims, F32)

    return pl.pallas_call(
        kernel,
        out_shape=jax.ShapeDtypeStruct(shape, BF16),
        in_specs=[VMEM, VMEM, pl.BlockSpec(memory_space=pl.ANY), SMEM],
        out_specs=VMEM,
        scratch_shapes=[
            f(2, FRAME, 128), f(CELLS, 128), f(FRAME, 128), f(FRAME, 128), bf(EXT, EXT, MODES),
            *[f(EXT + 4, EXT, MODES)] * 3,
            *[f(EXT + 4, FRAME, MODES)] * 4,
            bf(EXT, EXT, MODES), bf(EXT + 2, EXT, MODES),
            bf(17, EXT, MODES), bf(2, 17, 16, MODES), bf(56, 16, MODES), bf(56, 16, MODES),
            bf(EXT, MODES), bf(EXT, MODES), bf(80, MODES), bf(80, MODES),
            bf(2, 32, MODES), bf(2, 32, MODES), bf(2, 32, MODES),
            bf(5, MODES, MODES), bf(5, MODES, MODES), bf(*shape), bf(3, 2, 2, 16, MODES),
            dma, dma((8,)), dma((8,)), dma((19,)), dma((19,)), dma((5,)), dma((5,)),
            dma((3, cols)), dma((3, cols)),
            dma((3, 2, PLANE)), dma((3, 2, PLANE)), dma((3, 2)), dma((3, 2)),
        ],
        compiler_params=pltpu.CompilerParams(
            collective_id=0, has_side_effects=True, vmem_limit_bytes=60 * 2**20
        ),
    )(conductivity, storage, modes, owners)


def spread_kernel(got_ref, self_ref, cross_ref):
    most = got_ref.shape[2] // 8
    for source in range(got_ref.shape[0]):
        for slot, s in enumerate(ORDER):
            x = got_ref[source, slot].astype(F32)
            for rank in range(most):
                part = x[8 * rank : 8 * rank + 8]
                if s is None:
                    self_ref[0, source * most + rank] = part
                else:
                    cross_ref[0, source * most + rank, s] = part


def spread(got, slots):
    return pl.pallas_call(
        spread_kernel,
        out_shape=(
            jax.ShapeDtypeStruct((1, slots, 8, MODES), F32),
            jax.ShapeDtypeStruct((1, slots, 8, 8, MODES), F32),
        ),
        in_specs=[VMEM],
        out_specs=(VMEM, VMEM),
    )(got)


def on_device(modes, conductivity, storage, owners, slots, cols):
    got = assemble(conductivity, storage, modes, owners.reshape(1, GROUPS), cols, slots)
    return spread(got, slots)


def solution(mesh):
    cols = mesh.shape["col"]
    return jax.shard_map(
        functools.partial(on_device, slots=2 * cols, cols=cols),
        mesh=mesh,
        in_specs=(
            P("row", "col", None),
            P("row", "col"),
            P("row", "col"),
            P("row", "col", None, None),
        ),
        out_specs=(P("row", "col", None, None), P("row", "col", None, None, None)),
        check_vma=False,
    )
```
